512 devices in a mesh: ctx: 64 (over z, y), tp: 8 (over x, core).
Axes of the slice: x: 4, y: 8, z: 8, core: 2. Of those that a mesh axis runs over, the one named last changes fastest.
Arguments:
- queries: bfloat16 [2, 128, 128, 128], P(None, 'ctx', 'tp'), may hold values from -140 to 140
- key_codes: bfloat16 [8, 131072, 128], P('tp', 'ctx'), may hold values from -4.5 to 4.5
- key_scales: float32 [8, 131072], P('tp', 'ctx'), may hold values from 0.5 to 3
- value_codes: bfloat16 [8, 131072, 128], P('tp', 'ctx'), may hold values from -4 to 4
- value_scales: float32 [8, 131072], P('tp', 'ctx'), may hold values from 0.25 to 2
- lengths: int32 [128], replicated, may hold values from 65536 to 131072
- out_weight: bfloat16 [16384, 16384], P('tp', 'ctx'), may hold values from -0.046875 to 0.046875
Outputs:
- projected: bfloat16 [2, 128, 16384], P(None, 'tp', 'ctx')
The draws below stay inside these ranges and needn't reach their ends.
All inputs are finite; a program needn't handle non-finite values.
Results may differ from the reference program's by a relative error of at most 0.023.
Values may be sent and summed in bfloat16 or wider, within the bound.
No kernel may reach another device: no remote copies, remote signals or barrier semaphores. Data moves between devices by JAX's collectives and lax.ppermute only.
A program may use at most 64 MiB of HBM per device.

```python
import math
import jax
import jax.numpy as jnp
from jax import lax

D = 16384
KVH = 8
HPG = 16
HD = 128
STEPS = 2
MEM_DEV = 2048
HQ = 128
ROWS = 128
MEM = 131072


def shared_memory(key):
    code_key = jax.random.fold_in(key, 11)
    codes = jnp.clip(jax.random.normal(code_key, (KVH, MEM, HD), jnp.float32), -4.0, 4.0)
    return codes


def draw_key_codes(key, part):
    codes = shared_memory(key)
    return codes.astype(jnp.bfloat16)


def draw_key_scales(key, part):
    key = jax.random.fold_in(key, 2)
    logs = jax.random.uniform(key, (KVH, MEM), jnp.float32, jnp.log(0.5), jnp.log(3.0))
    return jnp.exp(logs).astype(jnp.float32)


def draw_queries(key, part):
    key = jax.random.fold_in(key, 3)
    values = 1.5 * jax.random.normal(key, (STEPS, ROWS, KVH * HPG, HD), jnp.float32)
    return jnp.clip(values, -9.0, 9.0).astype(jnp.bfloat16)


def draw_lengths(key, part):
    key = jax.random.fold_in(key, 4)
    first_key = jax.random.fold_in(key, 1)
    second_key = jax.random.fold_in(key, 2)
    values = jax.random.randint(first_key, (ROWS,), MEM // 2, MEM + 1)
    which = jax.random.randint(second_key, (), 0, ROWS)
    return jnp.where(jnp.arange(ROWS) == which, MEM, values).astype(jnp.int32)


def levels(own_key, extent, pieces, smallest, top_value):
    gain = 1.0
    for axis_at, parts in pieces:
        steps = jax.random.uniform(jax.random.fold_in(jax.random.fold_in(own_key, 6), axis_at), (parts,), jnp.float32, smallest / len(pieces), top_value / len(pieces))
        gain = gain * jnp.repeat(jnp.exp(steps), extent[axis_at] // parts).reshape((-1,) + (1,) * (len(extent) - 1 - axis_at))
    return gain


def bell_draw(stream_key, dims, spread, bound, cuts=(), kind=jnp.bfloat16):
    array = jax.random.normal(stream_key, dims, jnp.float32) * spread
    if len(cuts) > 0:
        array = levels(stream_key, dims, cuts, -0.22, 0.18) * array
    return jnp.clip(array, min=-bound, max=bound).astype(kind)


def setup_inputs(seed: int = 0) -> dict:
    seeds = jax.random.split(jax.random.key(seed), 8)
    queries = draw_queries(jax.random.fold_in(seeds[7], 71), 0)
    key_codes = draw_key_codes(jax.random.fold_in(seeds[7], 71), 0)
    key_scales = draw_key_scales(jax.random.fold_in(seeds[7], 71), 0)
    value_codes = bell_draw(seeds[3], (KVH, MEM, HD), 1.0, 4.0, ((0, 8), (1, 64)))
    value_scales = jnp.clip(jnp.exp(math.log(2.0) - 2.0794415 * jax.random.uniform(seeds[4], (KVH, MEM), jnp.float32) ** levels(seeds[4], (KVH, MEM), ((0, 8), (1, 64)), -0.2, 0.2)), 0.25, 2.0)
    lengths = draw_lengths(jax.random.fold_in(seeds[7], 71), 0)
    out_weight = bell_draw(seeds[6], (HQ * HD, D), (HQ * HD) ** -0.5, 0.046875, ((0, 8), (1, 64)))
    return dict(queries=queries, key_codes=key_codes, key_scales=key_scales, value_codes=value_codes, value_scales=value_scales, lengths=lengths, out_weight=out_weight)


def hadamard_signs(order):
    position = jnp.arange(order, dtype=jnp.int32)
    common = jnp.bitwise_and(position[:, None], position[None, :])
    parity = jnp.zeros((order, order), jnp.int32)
    for shift_by in range(order.bit_length() - 1):
        parity = parity + jnp.bitwise_and(jnp.right_shift(common, shift_by), 1)
    return (1 - 2 * (parity % 2)).astype(jnp.float32)

def reference(queries, key_codes, key_scales, value_codes, value_scales, lengths, out_weight):
    step_total, row_total, head_total, width = queries.shape
    group_total, memory_total = (key_codes.shape[0], key_codes.shape[1])
    per_group = head_total // group_total
    block_size = MEM_DEV
    block_total = memory_total // block_size
    inverse_square_root = 1.0 / math.sqrt(width)
    token = jnp.arange(memory_total, dtype=jnp.int32)
    block_rows = math.gcd(row_total, 16)
    block_count = row_total // block_rows
    grouped = jnp.moveaxis(queries.reshape(step_total, row_total, group_total, per_group, width), 2, 0)
    limit_blocks = lengths.reshape(block_count, block_rows)

    def one_group(group_within):
        query_per_group, key_codes_per_group, key_scale_per_group, value_codes_per_group, value_scale_per_group = group_within
        query_blocks = jnp.moveaxis(query_per_group.reshape(step_total, block_count, block_rows, per_group, width), 1, 0)
        vcodes_split = value_codes_per_group.astype(jnp.float32).reshape(block_total, block_size, width)

        def one_block(block_in):
            query_block, limit = block_in
            unscaled_logits = jnp.einsum('srpd,md->srpm', query_block.astype(jnp.float32), key_codes_per_group.astype(jnp.float32))
            score_logits = unscaled_logits * (key_scale_per_group * inverse_square_root)[None, None, None, :]
            valid = (token[None, :] < limit[:, None])[None, :, None, :]
            masked = jnp.where(valid, score_logits, -1e+30)
            shape_split = (step_total, block_rows, per_group, block_total, block_size)
            masked = masked.reshape(shape_split)
            valid_split = jnp.broadcast_to(valid, score_logits.shape).reshape(shape_split)
            top = lax.optimization_barrier(jnp.max(masked, axis=-1))
            expo = jnp.where(valid_split, jnp.exp(masked - top[..., None]), 0.0)
            total = lax.optimization_barrier(jnp.sum(expo, axis=-1))
            weights = (expo * value_scale_per_group.reshape(block_total, block_size)[None, None, None]).astype(jnp.bfloat16)
            summed = jnp.einsum('srpbm,bmd->srpbd', weights.astype(jnp.float32), vcodes_split)
            peak = lax.optimization_barrier(jnp.max(top, axis=-1))
            factor = jnp.exp(top - peak[..., None])
            part = summed * factor[..., None]
            part_total = total * factor
            return lax.optimization_barrier(jnp.sum(part, axis=3)) / lax.optimization_barrier(jnp.sum(part_total, axis=3))[..., None]
        result = lax.map(one_block, (query_blocks, limit_blocks))
        return jnp.moveaxis(result, 0, 1).reshape(step_total, row_total, per_group, width)
    rotated = lax.map(one_group, (grouped, key_codes, key_scales, value_codes, value_scales))
    rotated = jnp.moveaxis(rotated, 0, 2).reshape(step_total * row_total * head_total, width)
    signs = hadamard_signs(width)
    attended = jnp.dot(rotated, signs, precision=lax.Precision.HIGHEST, preferred_element_type=jnp.float32) * inverse_square_root
    attended = attended.astype(jnp.bfloat16).reshape(step_total * row_total, head_total * width)
    projected = jnp.dot(attended, out_weight, preferred_element_type=jnp.float32)
    return projected.astype(jnp.bfloat16).reshape(step_total, row_total, out_weight.shape[1])
```

```python
import functools
import math

import jax
import jax.numpy as jnp
from jax import lax
from jax.experimental import pallas as pl
from jax.experimental.pallas import tpu as pltpu
from jax.sharding import PartitionSpec as P

F32 = jnp.float32
BF16 = jnp.bfloat16
LOG2E = 1.0 / math.log(2.0)
EXTRA = 8
NONE = -(2.0**100)


def split_two(x):
    high = x.astype(BF16).astype(F32)
    low = (x - high).astype(BF16).astype(F32)
    return high, low


def iota(shape, axis):
    return lax.broadcasted_iota(jnp.int32, shape, axis)


def attention_kernel(len_ref, q_ref, kt_ref, kf_ref, v_ref, out_ref, s_ref, p_ref, m_ref):
    sources, vectors, width = q_ref.shape
    tokens = kt_ref.shape[1]
    rows = sources * vectors
    group = pl.program_id(0)
    place = lax.axis_index("ctx")
    q = q_ref[...].reshape(rows, width)
    s_ref[...] = jnp.dot(q, kt_ref[...], preferred_element_type=F32)
    kf = kf_ref[...]
    token = place * tokens + iota((1, tokens), 1)
    sub = 16
    lane = iota((sub, width), 1)
    odd = iota((sub, 1), 0) % 2
    for at in range(0, rows, sub):
        own = group * (2 * sources) + 2 * (at // vectors)
        limit = jnp.where(odd == 0, len_ref[own], len_ref[own + 1])
        score = jnp.where(token < limit, s_ref[at : at + sub, :] * kf, NONE)
        high, low = split_two(jnp.max(score, axis=1, keepdims=True))
        p_ref[at : at + sub, :] = jnp.exp2(score - (high + low)).astype(BF16)
        m_ref[at : at + sub, :] = jnp.where(lane == 0, high, low)
    sums = jnp.dot(p_ref[...], v_ref[...], preferred_element_type=F32)
    high, low = split_two(sums[:, width:])
    lane = iota((rows, width), 1)
    extra = jnp.where(lane < 2, m_ref[...], jnp.where(lane == 2, high, low))
    pick = (iota((EXTRA, width), 0) == iota((EXTRA, width), 1)).astype(BF16)
    parts = vectors // 8
    pad = jnp.zeros((width - sources * 8, width), BF16)
    for part in range(parts):
        places = [source * vectors + part * 8 for source in range(sources)]
        block = jnp.concatenate([sums[at : at + 8, :width] for at in places], axis=0)
        out_ref[part, : sources * 8, :] = block.astype(BF16)
        block = jnp.concatenate([extra[at : at + 8, :] for at in places], axis=0).astype(BF16)
        block = jnp.concatenate([block, pad], axis=0)
        turned = lax.dot_general(pick, block, (((1,), (1,)), ((), ())), preferred_element_type=F32)
        out_ref[part, sources * 8 :, :] = turned.astype(BF16)


def combine_kernel(in_ref, out_ref):
    places, total_rows, width = in_ref.shape
    vectors = total_rows - EXTRA
    extra = in_ref[:, vectors:, :].astype(F32).reshape(places * EXTRA, width).astype(BF16)
    unit = (iota((vectors, width), 0) == iota((vectors, width), 1)).astype(BF16)
    turned = lax.dot_general(unit, extra, (((1,), (1,)), ((), ())), preferred_element_type=F32)
    turned = turned.astype(BF16)
    column = iota((places * EXTRA, places), 0)
    wanted = iota((places * EXTRA, places), 1) * EXTRA

    def kind(index):
        pick = (column == wanted + index).astype(BF16)
        return jnp.dot(turned, pick, preferred_element_type=F32)

    top = kind(0) + kind(1)
    total = kind(2) + kind(3)
    factor = jnp.exp2(top - jnp.max(top, axis=1, keepdims=True))
    denom = jnp.sum(factor * total, axis=1, keepdims=True)
    numer = jnp.zeros((vectors, width), F32)
    for at in range(places):
        numer = numer + factor[:, at : at + 1] * in_ref[at, :vectors, :].astype(F32)
    rotated = numer / denom
    common = iota((width, width), 0) & iota((width, width), 1)
    common = common ^ (common >> 4)
    common = common ^ (common >> 2)
    common = common ^ (common >> 1)
    signs = (1 - 2 * (common & 1)).astype(F32)
    attended = jnp.dot(rotated, signs, precision=lax.Precision.HIGHEST, preferred_element_type=F32)
    attended = (attended * (1.0 / math.sqrt(width))).astype(BF16)
    new = iota((vectors, vectors), 0)
    old = iota((vectors, vectors), 1)
    source = (new % 16) // 2
    pick = (old == source * 8 + (new // 16) * 2 + new % 2).astype(BF16)
    attended = jnp.dot(pick, attended, preferred_element_type=F32).astype(BF16)
    for at in range(places):
        out_ref[at] = attended


def project_kernel(in_ref, w_ref, out_ref):
    groups, pairs, vectors, width = in_ref.shape
    half = vectors // 2
    terms = jnp.zeros((groups * half, w_ref.shape[1]), F32)
    for pair in range(pairs):
        both = [
            in_ref[:, pair, at : at + half, :].reshape(groups * half, width) for at in (0, half)
        ]
        terms = terms + jnp.dot(
            jnp.concatenate(both, axis=1),
            w_ref[pair * 2 * width : (pair + 1) * 2 * width, :],
            preferred_element_type=F32,
        )
    out_ref[...] = terms.astype(BF16).reshape(out_ref.shape)


def local(queries, key_codes, key_scales, value_codes, value_scales, lengths, out_weight):
    steps, rows_own, heads, width = queries.shape
    tokens = key_codes.shape[1]
    places = lax.axis_size("ctx")
    groups = lax.axis_size("tp")
    sources = places // groups
    vectors = steps * rows_own * heads

    own = queries.transpose(2, 0, 1, 3).reshape(1, vectors, width)
    query = lax.all_to_all(
        jnp.broadcast_to(own, (places, vectors, width)), "ctx", 0, 0, tiled=True
    )
    key_turned = key_codes[0].T
    key_factor = key_scales * (LOG2E / math.sqrt(width))
    value = (value_codes[0].astype(F32) * value_scales[0][:, None]).astype(BF16)
    value = jnp.concatenate([value, jnp.ones_like(value)], axis=1)

    block = sources * vectors
    whole = lambda *shape: pl.BlockSpec(shape, lambda i: (0,) * len(shape))
    partial = pl.pallas_call(
        attention_kernel,
        grid=(groups,),
        out_shape=jax.ShapeDtypeStruct((places, vectors + EXTRA, width), BF16),
        in_specs=[
            pl.BlockSpec(memory_space=pltpu.SMEM),
            pl.BlockSpec((sources, vectors, width), lambda i: (i, 0, 0)),
            whole(width, tokens),
            whole(1, tokens),
            whole(tokens, 2 * width),
        ],
        out_specs=pl.BlockSpec((sources, vectors + EXTRA, width), lambda i: (i, 0, 0)),
        scratch_shapes=[
            pltpu.VMEM((block, tokens), F32),
            pltpu.VMEM((block, tokens), BF16),
            pltpu.VMEM((block, width), F32),
        ],
        compiler_params=pltpu.CompilerParams(vmem_limit_bytes=48 * 1024 * 1024),
        cost_estimate=pl.CostEstimate(
            flops=8 * places * vectors * tokens * width,
            bytes_accessed=8 * 1024 * 1024,
            transcendentals=places * vectors * tokens,
        ),
        name="attention",
    )(lengths, query, key_turned, key_factor, value)

    pieces = lax.all_to_all(partial, "ctx", 0, 0, tiled=True)
    params = pltpu.CompilerParams(vmem_limit_bytes=32 * 1024 * 1024)
    attended = pl.pallas_call(
        combine_kernel,
        out_shape=jax.ShapeDtypeStruct((places, vectors, width), BF16),
        compiler_params=params,
        name="combine",
    )(pieces)
    attended = lax.all_to_all(attended, "ctx", 0, 0, tiled=True)
    half = vectors // 2
    terms = pl.pallas_call(
        project_kernel,
        out_shape=jax.ShapeDtypeStruct((groups, half, out_weight.shape[1]), BF16),
        compiler_params=params,
        name="project",
    )(attended.reshape(groups, sources, vectors, width), out_weight)
    terms = lax.all_to_all(terms, "tp", 0, 0, tiled=True)
    projected = jnp.sum(terms.astype(F32), axis=0).astype(BF16)
    return projected.reshape(steps, half // steps, out_weight.shape[1])


def solution(mesh):
    return jax.shard_map(
        local,
        mesh=mesh,
        in_specs=(
            P(None, "ctx", "tp", None),
            P("tp", "ctx", None),
            P("tp", "ctx"),
            P("tp", "ctx", None),
            P("tp", "ctx"),
            P(),
            P("tp", "ctx"),
        ),
        out_specs=P(None, "tp", "ctx"),
        check_vma=False,
    )
```

```python
import functools
import math

import jax
import jax.numpy as jnp
from jax import lax
from jax.experimental import pallas as pl
from jax.experimental.pallas import tpu as pltpu
from jax.sharding import PartitionSpec as P

F32 = jnp.float32
BF16 = jnp.bfloat16
LOG2E = 1.0 / math.log(2.0)
EXTRA = 8
NONE = -(2.0**100)


def split_two(x):
    high = x.astype(BF16).astype(F32)
    low = (x - high).astype(BF16).astype(F32)
    return high, low


def iota(shape, axis):
    return lax.broadcasted_iota(jnp.int32, shape, axis)


def attention_kernel(
    len_ref, q_ref, kt_ref, kf_ref, v_ref, out_ref, s_even, s_odd, p_even, p_odd, m_even, m_odd
):
    vectors, width = q_ref.shape[1:]
    tokens = kt_ref.shape[1]
    rows = s_even.shape[0]
    sources = rows // vectors
    groups = q_ref.shape[0] // sources
    parts = vectors // 8
    sub = 16
    start = lax.axis_index("ctx") * tokens
    scores, weights, marks = (s_even, s_odd), (p_even, p_odd), (m_even, m_odd)

    def limits(group, source):
        row = (group * sources + source) * 2
        return len_ref[row] - start, len_ref[row + 1] - start

    def score(group, slot):
        q = q_ref[pl.ds(group * sources, sources)].reshape(rows, width)
        scores[slot][...] = jnp.dot(q, kt_ref[...], preferred_element_type=F32)

    def mask(group, slot):
        for source in range(sources):
            even, odd = limits(group, source)
            inside = ((even > 0) & (even < tokens)) | ((odd > 0) & (odd < tokens))

            @pl.when(inside)
            def _():
                first = jnp.where(even <= 0, tokens, even)
                second = jnp.where(odd <= 0, tokens, odd)
                limit = jnp.where(iota((sub, 1), 0) % 2 == 0, first, second)
                valid = iota((1, tokens), 1) < limit
                for at in range(source * vectors, (source + 1) * vectors, sub):
                    held = scores[slot][at : at + sub, :]
                    scores[slot][at : at + sub, :] = jnp.where(valid, held, NONE)

    def weigh(group, slot):
        kf = kf_ref[...]
        lane = iota((sub, width), 1)
        for at in range(0, rows, sub):
            even, odd = limits(group, at // vectors)
            some = jnp.where(iota((sub, 1), 0) % 2 == 0, even, odd) > 0
            scaled = scores[slot][at : at + sub, :] * kf
            high, low = split_two(jnp.max(scaled, axis=1, keepdims=True))
            weights[slot][at : at + sub, :] = jnp.exp2(scaled - (high + low)).astype(BF16)
            high = jnp.where(some, high, NONE)
            low = jnp.where(some, low, 0.0)
            marks[slot][at : at + sub, :] = jnp.where(lane == 0, high, low)

    def gather(group, slot):
        sums = jnp.dot(weights[slot][...], v_ref[...], preferred_element_type=F32)
        high, low = split_two(sums[:, width:])
        lane = iota((rows, width), 1)
        extra = jnp.where(lane < 2, marks[slot][...], jnp.where(lane == 2, high, low))
        extras = []
        for part in range(parts):
            places = [source * vectors + part * 8 for source in range(sources)]
            block = jnp.concatenate([sums[at : at + 8, :width] for at in places], axis=0)
            out_ref[group * parts + part, :vectors, :] = block.astype(BF16)
            extras += [extra[at : at + 8, :] for at in places]
        extras = jnp.concatenate(extras, axis=0).astype(BF16)
        pick = (iota((EXTRA, width), 0) == iota((EXTRA, width), 1)).astype(BF16)
        turned = lax.dot_general(pick, extras, (((1,), (1,)), ((), ())), preferred_element_type=F32)
        for part in range(parts):
            at = part // 2 * width
            row = turned[:, at : at + width]
            if part % 2:
                row = pltpu.roll(row, vectors, 1)
            out_ref[group * parts + part, vectors:, :] = row.astype(BF16)

    def step(group, slot):
        mask(group - 1, 1 - slot)
        score(group, slot)
        weigh(group - 1, 1 - slot)
        gather(group - 1, 1 - slot)

    def pair(index, carry):
        step(2 * index, 0)
        step(2 * index + 1, 1)
        return carry

    score(0, 0)
    step(1, 1)
    lax.fori_loop(1, groups // 2, pair, 0)
    mask(groups - 1, 1)
    weigh(groups - 1, 1)
    gather(groups - 1, 1)


def combine_kernel(in_ref, out_ref):
    places, total_rows, width = in_ref.shape
    vectors = total_rows - EXTRA
    extra = in_ref[:, vectors:, :].astype(F32).reshape(places * EXTRA, width).astype(BF16)
    unit = (iota((vectors, width), 0) == iota((vectors, width), 1)).astype(BF16)
    turned = lax.dot_general(unit, extra, (((1,), (1,)), ((), ())), preferred_element_type=F32)
    turned = turned.astype(BF16)
    column = iota((places * EXTRA, places), 0)
    wanted = iota((places * EXTRA, places), 1) * EXTRA

    def kind(index):
        pick = (column == wanted + index).astype(BF16)
        return jnp.dot(turned, pick, preferred_element_type=F32)

    top = kind(0) + kind(1)
    total = kind(2) + kind(3)
    factor = jnp.exp2(top - jnp.max(top, axis=1, keepdims=True))
    denom = jnp.sum(factor * total, axis=1, keepdims=True)
    numer = jnp.zeros((vectors, width), F32)
    for at in range(places):
        numer = numer + factor[:, at : at + 1] * in_ref[at, :vectors, :].astype(F32)
    rotated = numer / denom
    common = iota((width, width), 0) & iota((width, width), 1)
    common = common ^ (common >> 4)
    common = common ^ (common >> 2)
    common = common ^ (common >> 1)
    signs = (1 - 2 * (common & 1)).astype(F32)
    attended = jnp.dot(rotated, signs, precision=lax.Precision.HIGHEST, preferred_element_type=F32)
    attended = (attended * (1.0 / math.sqrt(width))).astype(BF16)
    new = iota((vectors, vectors), 0)
    old = iota((vectors, vectors), 1)
    source = (new % 16) // 2
    pick = (old == source * 8 + (new // 16) * 2 + new % 2).astype(BF16)
    attended = jnp.dot(pick, attended, preferred_element_type=F32).astype(BF16)
    for at in range(places):
        out_ref[at] = attended


def project_kernel(in_ref, w_ref, out_ref):
    groups, pairs, vectors, width = in_ref.shape
    half = vectors // 2
    terms = jnp.zeros((groups * half, w_ref.shape[1]), F32)
    for pair in range(pairs):
        both = [
            in_ref[:, pair, at : at + half, :].reshape(groups * half, width) for at in (0, half)
        ]
        terms = terms + jnp.dot(
            jnp.concatenate(both, axis=1),
            w_ref[pair * 2 * width : (pair + 1) * 2 * width, :],
            preferred_element_type=F32,
        )
    out_ref[...] = terms.astype(BF16).reshape(out_ref.shape)


def local(queries, key_codes, key_scales, value_codes, value_scales, lengths, out_weight):
    steps, rows_own, heads, width = queries.shape
    tokens = key_codes.shape[1]
    places = lax.axis_size("ctx")
    groups = lax.axis_size("tp")
    sources = places // groups
    vectors = steps * rows_own * heads

    own = queries.transpose(2, 0, 1, 3).reshape(1, vectors, width)

    def direct(own):
        return lax.all_to_all(
            jnp.broadcast_to(own, (places, vectors, width)), "ctx", 0, 0, tiled=True
        )

    def two_stages(own):
        lines = [[at * sources + i for i in range(sources)] for at in range(groups)]
        across = [[i * sources + at for i in range(groups)] for at in range(sources)]
        line = lax.all_to_all(
            jnp.broadcast_to(own, (sources, vectors, width)),
            "ctx", 0, 0, axis_index_groups=lines, tiled=True,
        )
        line = line.reshape(1, sources * vectors, width)
        whole = lax.all_to_all(
            jnp.broadcast_to(line, (groups, sources * vectors, width)),
            "ctx", 0, 0, axis_index_groups=across, tiled=True,
        )
        return whole.reshape(places, vectors, width)

    def prepare(key_codes, key_scales, value_codes, value_scales):
        value = (value_codes[0].astype(F32) * value_scales[0][:, None]).astype(BF16)
        value = jnp.concatenate([value, jnp.ones_like(value)], axis=1)
        return key_codes[0].T, key_scales * (LOG2E / math.sqrt(width)), value

    memory = (key_codes, key_scales, value_codes, value_scales)
    query, (key_turned, key_factor, value) = lax.cond(
        lax.axis_index("tp") % 2 == 0,
        lambda own, memory: (direct(own), prepare(*memory)),
        lambda own, memory: (two_stages(own), prepare(*memory)),
        own,
        memory,
    )

    block = sources * vectors
    vmem = pl.BlockSpec(memory_space=pltpu.VMEM)
    partial = pl.pallas_call(
        attention_kernel,
        out_shape=jax.ShapeDtypeStruct((places, vectors + EXTRA, width), BF16),
        in_specs=[pl.BlockSpec(memory_space=pltpu.SMEM), vmem, vmem, vmem, vmem],
        out_specs=vmem,
        scratch_shapes=[pltpu.VMEM((block, tokens), F32)] * 2
        + [pltpu.VMEM((block, tokens), BF16)] * 2
        + [pltpu.VMEM((block, width), F32)] * 2,
        compiler_params=pltpu.CompilerParams(vmem_limit_bytes=48 * 1024 * 1024),
        cost_estimate=pl.CostEstimate(
            flops=8 * places * vectors * tokens * width,
            bytes_accessed=8 * 1024 * 1024,
            transcendentals=places * vectors * tokens,
        ),
        name="attention",
    )(lengths, query, key_turned, key_factor, value)

    pieces = lax.all_to_all(partial, "ctx", 0, 0, tiled=True)
    params = pltpu.CompilerParams(vmem_limit_bytes=32 * 1024 * 1024)
    attended = pl.pallas_call(
        combine_kernel,
        out_shape=jax.ShapeDtypeStruct((places, vectors, width), BF16),
        compiler_params=params,
        name="combine",
    )(pieces)
    attended = lax.all_to_all(attended, "ctx", 0, 0, tiled=True)
    half = vectors // 2
    terms = pl.pallas_call(
        project_kernel,
        out_shape=jax.ShapeDtypeStruct((groups, half, out_weight.shape[1]), BF16),
        compiler_params=params,
        name="project",
    )(attended.reshape(groups, sources, vectors, width), out_weight)
    terms = lax.all_to_all(terms, "tp", 0, 0, tiled=True)
    projected = jnp.sum(terms.astype(F32), axis=0).astype(BF16)
    return projected.reshape(steps, half // steps, out_weight.shape[1])


def solution(mesh):
    return jax.shard_map(
        local,
        mesh=mesh,
        in_specs=(
            P(None, "ctx", "tp", None),
            P("tp", "ctx", None),
            P("tp", "ctx"),
            P("tp", "ctx", None),
            P("tp", "ctx"),
            P(),
            P("tp", "ctx"),
        ),
        out_specs=P(None, "tp", "ctx"),
        check_vma=False,
    )
```

```python
import functools
import math

import jax
import jax.numpy as jnp
from jax import lax
from jax.experimental import pallas as pl
from jax.experimental.pallas import tpu as pltpu
from jax.sharding import PartitionSpec as P

F32 = jnp.float32
BF16 = jnp.bfloat16
LOG2E = 1.0 / math.log(2.0)
EXTRA = 8
NONE = -(2.0**100)


def split_two(x):
    high = x.astype(BF16).astype(F32)
    low = (x - high).astype(BF16).astype(F32)
    return high, low


def iota(shape, axis):
    return lax.broadcasted_iota(jnp.int32, shape, axis)


def attention_kernel(
    len_ref, q_ref, kt_ref, kf_ref, v_ref, out_ref, s_even, s_odd, p_even, p_odd, m_even, m_odd
):
    vectors, width = q_ref.shape[1:]
    tokens = kt_ref.shape[1]
    rows = s_even.shape[0]
    sources = rows // vectors
    groups = q_ref.shape[0] // sources
    parts = vectors // 8
    sub = 16
    start = lax.axis_index("ctx") * tokens
    scores, weights, marks = (s_even, s_odd), (p_even, p_odd), (m_even, m_odd)

    def limits(group, source):
        row = (group * sources + source) * 2
        return len_ref[row] - start, len_ref[row + 1] - start

    def score(group, slot):
        q = q_ref[pl.ds(group * sources, sources)].reshape(rows, width)
        scores[slot][...] = jnp.dot(q, kt_ref[...], preferred_element_type=F32)

    def mask(group, slot):
        for source in range(sources):
            even, odd = limits(group, source)
            inside = ((even > 0) & (even < tokens)) | ((odd > 0) & (odd < tokens))

            @pl.when(inside)
            def _():
                first = jnp.where(even <= 0, tokens, even)
                second = jnp.where(odd <= 0, tokens, odd)
                limit = jnp.where(iota((sub, 1), 0) % 2 == 0, first, second)
                valid = iota((1, tokens), 1) < limit
                for at in range(source * vectors, (source + 1) * vectors, sub):
                    held = scores[slot][at : at + sub, :]
                    scores[slot][at : at + sub, :] = jnp.where(valid, held, NONE)

    def weigh(group, slot, half):
        kf = kf_ref[...]
        lane = iota((sub, width), 1)
        for at in range(half * rows // 2, (half + 1) * rows // 2, sub):
            even, odd = limits(group, at // vectors)
            some = jnp.where(iota((sub, 1), 0) % 2 == 0, even, odd) > 0
            scaled = scores[slot][at : at + sub, :] * kf
            high, low = split_two(jnp.max(scaled, axis=1, keepdims=True))
            weights[slot][at : at + sub, :] = jnp.exp2(scaled - (high + low)).astype(BF16)
            high = jnp.where(some, high, NONE)
            low = jnp.where(some, low, 0.0)
            marks[slot][at : at + sub, :] = jnp.where(lane == 0, high, low)

    def sums_of(slot, half):
        own = weights[slot][half * rows // 2 : (half + 1) * rows // 2, :]
        return jnp.dot(own, v_ref[...], preferred_element_type=F32)

    def finish(group, slot):
        weigh(group, slot, 0)
        first = sums_of(slot, 0)
        weigh(group, slot, 1)
        sums = jnp.concatenate([first, sums_of(slot, 1)], axis=0)
        high, low = split_two(sums[:, width:])
        lane = iota((rows, width), 1)
        extra = jnp.where(lane < 2, marks[slot][...], jnp.where(lane == 2, high, low))
        extras = []
        for part in range(parts):
            places = [source * vectors + part * 8 for source in range(sources)]
            block = jnp.concatenate([sums[at : at + 8, :width] for at in places], axis=0)
            out_ref[group * parts + part, :vectors, :] = block.astype(BF16)
            extras += [extra[at : at + 8, :] for at in places]
        extras = jnp.concatenate(extras, axis=0).astype(BF16)
        pick = (iota((EXTRA, width), 0) == iota((EXTRA, width), 1)).astype(BF16)
        turned = lax.dot_general(pick, extras, (((1,), (1,)), ((), ())), preferred_element_type=F32)
        for part in range(parts):
            at = part // 2 * width
            row = turned[:, at : at + width]
            if part % 2:
                row = pltpu.roll(row, vectors, 1)
            out_ref[group * parts + part, vectors:, :] = row.astype(BF16)

    def step(group, slot):
        mask(group - 1, 1 - slot)
        score(group, slot)
        finish(group - 1, 1 - slot)

    def pair(index, carry):
        step(2 * index, 0)
        step(2 * index + 1, 1)
        return carry

    score(0, 0)
    step(1, 1)
    lax.fori_loop(1, groups // 2, pair, 0)
    mask(groups - 1, 1)
    finish(groups - 1, 1)


def combine_kernel(in_ref, out_ref):
    places, total_rows, width = in_ref.shape
    vectors = total_rows - EXTRA
    extra = in_ref[:, vectors:, :].astype(F32).reshape(places * EXTRA, width).astype(BF16)
    unit = (iota((vectors, width), 0) == iota((vectors, width), 1)).astype(BF16)
    turned = lax.dot_general(unit, extra, (((1,), (1,)), ((), ())), preferred_element_type=F32)
    turned = turned.astype(BF16)
    column = iota((places * EXTRA, places), 0)
    wanted = iota((places * EXTRA, places), 1) * EXTRA

    def kind(index):
        pick = (column == wanted + index).astype(BF16)
        return jnp.dot(turned, pick, preferred_element_type=F32)

    top = kind(0) + kind(1)
    total = kind(2) + kind(3)
    factor = jnp.exp2(top - jnp.max(top, axis=1, keepdims=True))
    denom = jnp.sum(factor * total, axis=1, keepdims=True)
    numer = jnp.zeros((vectors, width), F32)
    for at in range(places):
        numer = numer + factor[:, at : at + 1] * in_ref[at, :vectors, :].astype(F32)
    rotated = numer / denom
    common = iota((width, width), 0) & iota((width, width), 1)
    common = common ^ (common >> 4)
    common = common ^ (common >> 2)
    common = common ^ (common >> 1)
    signs = (1 - 2 * (common & 1)).astype(F32)
    attended = jnp.dot(rotated, signs, precision=lax.Precision.HIGHEST, preferred_element_type=F32)
    attended = (attended * (1.0 / math.sqrt(width))).astype(BF16)
    new = iota((vectors, vectors), 0)
    old = iota((vectors, vectors), 1)
    source = (new % 16) // 2
    pick = (old == source * 8 + (new // 16) * 2 + new % 2).astype(BF16)
    attended = jnp.dot(pick, attended, preferred_element_type=F32).astype(BF16)
    for at in range(places):
        out_ref[at] = attended


def project_kernel(in_ref, w_ref, out_ref):
    groups, pairs, vectors, width = in_ref.shape
    half = vectors // 2
    terms = jnp.zeros((groups * half, w_ref.shape[1]), F32)
    for pair in range(pairs):
        both = [
            in_ref[:, pair, at : at + half, :].reshape(groups * half, width) for at in (0, half)
        ]
        terms = terms + jnp.dot(
            jnp.concatenate(both, axis=1),
            w_ref[pair * 2 * width : (pair + 1) * 2 * width, :],
            preferred_element_type=F32,
        )
    out_ref[...] = terms.astype(BF16).reshape(out_ref.shape)


def local(queries, key_codes, key_scales, value_codes, value_scales, lengths, out_weight):
    steps, rows_own, heads, width = queries.shape
    tokens = key_codes.shape[1]
    places = lax.axis_size("ctx")
    groups = lax.axis_size("tp")
    sources = places // groups
    vectors = steps * rows_own * heads

    own = queries.transpose(2, 0, 1, 3).reshape(1, vectors, width)

    def direct(own):
        return lax.all_to_all(
            jnp.broadcast_to(own, (places, vectors, width)), "ctx", 0, 0, tiled=True
        )

    def two_stages(own):
        lines = [[at * sources + i for i in range(sources)] for at in range(groups)]
        across = [[i * sources + at for i in range(groups)] for at in range(sources)]
        line = lax.all_to_all(
            jnp.broadcast_to(own, (sources, vectors, width)),
            "ctx", 0, 0, axis_index_groups=lines, tiled=True,
        )
        line = line.reshape(1, sources * vectors, width)
        whole = lax.all_to_all(
            jnp.broadcast_to(line, (groups, sources * vectors, width)),
            "ctx", 0, 0, axis_index_groups=across, tiled=True,
        )
        return whole.reshape(places, vectors, width)

    def prepare(key_codes, key_scales, value_codes, value_scales):
        value = (value_codes[0].astype(F32) * value_scales[0][:, None]).astype(BF16)
        value = jnp.concatenate([value, jnp.ones_like(value)], axis=1)
        return key_codes[0].T, key_scales * (LOG2E / math.sqrt(width)), value

    def two_stages_first(own, memory):
        query, memory = lax.optimization_barrier((two_stages(own), memory))
        return query, prepare(*memory)

    memory = (key_codes, key_scales, value_codes, value_scales)
    query, (key_turned, key_factor, value) = lax.cond(
        lax.axis_index("tp") % 2 == 0,
        lambda own, memory: (direct(own), prepare(*memory)),
        two_stages_first,
        own,
        memory,
    )

    block = sources * vectors
    vmem = pl.BlockSpec(memory_space=pltpu.VMEM)
    partial = pl.pallas_call(
        attention_kernel,
        out_shape=jax.ShapeDtypeStruct((places, vectors + EXTRA, width), BF16),
        in_specs=[pl.BlockSpec(memory_space=pltpu.SMEM), vmem, vmem, vmem, vmem],
        out_specs=vmem,
        scratch_shapes=[pltpu.VMEM((block, tokens), F32)] * 2
        + [pltpu.VMEM((block, tokens), BF16)] * 2
        + [pltpu.VMEM((block, width), F32)] * 2,
        compiler_params=pltpu.CompilerParams(vmem_limit_bytes=48 * 1024 * 1024),
        cost_estimate=pl.CostEstimate(
            flops=8 * places * vectors * tokens * width,
            bytes_accessed=8 * 1024 * 1024,
            transcendentals=places * vectors * tokens,
        ),
        name="attention",
    )(lengths, query, key_turned, key_factor, value)

    pieces = lax.all_to_all(partial, "ctx", 0, 0, tiled=True)
    params = pltpu.CompilerParams(vmem_limit_bytes=32 * 1024 * 1024)
    attended = pl.pallas_call(
        combine_kernel,
        out_shape=jax.ShapeDtypeStruct((places, vectors, width), BF16),
        compiler_params=params,
        name="combine",
    )(pieces)
    attended = lax.all_to_all(attended, "ctx", 0, 0, tiled=True)
    half = vectors // 2
    terms = pl.pallas_call(
        project_kernel,
        out_shape=jax.ShapeDtypeStruct((groups, half, out_weight.shape[1]), BF16),
        compiler_params=params,
        name="project",
    )(attended.reshape(groups, sources, vectors, width), out_weight)
    terms = lax.all_to_all(terms, "tp", 0, 0, tiled=True)
    projected = jnp.sum(terms.astype(F32), axis=0).astype(BF16)
    return projected.reshape(steps, half // steps, out_weight.shape[1])


def solution(mesh):
    return jax.shard_map(
        local,
        mesh=mesh,
        in_specs=(
            P(None, "ctx", "tp", None),
            P("tp", "ctx", None),
            P("tp", "ctx"),
            P("tp", "ctx", None),
            P("tp", "ctx"),
            P(),
            P("tp", "ctx"),
        ),
        out_specs=P(None, "tp", "ctx"),
        check_vma=False,
    )
```

```python
import functools
import math

import jax
import jax.numpy as jnp
from jax import lax
from jax.experimental import pallas as pl
from jax.experimental.pallas import tpu as pltpu
from jax.sharding import PartitionSpec as P

F32 = jnp.float32
BF16 = jnp.bfloat16
LOG2E = 1.0 / math.log(2.0)
EXTRA = 8
NONE = -(2.0**100)


def split_two(x):
    high = x.astype(BF16).astype(F32)
    low = (x - high).astype(BF16).astype(F32)
    return high, low


def iota(shape, axis):
    return lax.broadcasted_iota(jnp.int32, shape, axis)


def attention_kernel(
    len_ref, q_ref, kt_ref, kf_ref, v_ref, out_ref,
    s_even, s_odd, p_even, p_odd, m_even, m_odd, e_even, e_odd,
):
    vectors, width = q_ref.shape[1:]
    tokens = kt_ref.shape[1]
    rows = s_even.shape[0]
    sources = rows // vectors
    groups = q_ref.shape[0] // sources
    parts = vectors // 8
    sub = 16
    start = lax.axis_index("ctx") * tokens
    scores, weights, marks = (s_even, s_odd), (p_even, p_odd), (m_even, m_odd)
    extras_of = (e_even, e_odd)

    def limits(group, source):
        row = (group * sources + source) * 2
        return len_ref[row] - start, len_ref[row + 1] - start

    def score(group, slot):
        q = q_ref[pl.ds(group * sources, sources)].reshape(rows, width)
        scores[slot][...] = jnp.dot(q, kt_ref[...], preferred_element_type=F32)

    def mask(group, slot):
        for source in range(sources):
            even, odd = limits(group, source)
            inside = ((even > 0) & (even < tokens)) | ((odd > 0) & (odd < tokens))

            @pl.when(inside)
            def _():
                first = jnp.where(even <= 0, tokens, even)
                second = jnp.where(odd <= 0, tokens, odd)
                limit = jnp.where(iota((sub, 1), 0) % 2 == 0, first, second)
                valid = iota((1, tokens), 1) < limit
                for at in range(source * vectors, (source + 1) * vectors, sub):
                    held = scores[slot][at : at + sub, :]
                    scores[slot][at : at + sub, :] = jnp.where(valid, held, NONE)

    def weigh(group, slot, half):
        kf = kf_ref[...]
        lane = iota((sub, width), 1)
        for at in range(half * rows // 2, (half + 1) * rows // 2, sub):
            even, odd = limits(group, at // vectors)
            some = jnp.where(iota((sub, 1), 0) % 2 == 0, even, odd) > 0
            scaled = scores[slot][at : at + sub, :] * kf
            high, low = split_two(jnp.max(scaled, axis=1, keepdims=True))
            weights[slot][at : at + sub, :] = jnp.exp2(scaled - (high + low)).astype(BF16)
            high = jnp.where(some, high, NONE)
            low = jnp.where(some, low, 0.0)
            marks[slot][at : at + sub, :] = jnp.where(lane == 0, high, low)

    def sums_of(slot, half):
        own = weights[slot][half * rows // 2 : (half + 1) * rows // 2, :]
        return jnp.dot(own, v_ref[...], preferred_element_type=F32)

    def finish(group, slot):
        weigh(group, slot, 0)
        first = sums_of(slot, 0)
        weigh(group, slot, 1)
        sums = jnp.concatenate([first, sums_of(slot, 1)], axis=0)
        high, low = split_two(sums[:, width:])
        lane = iota((rows, width), 1)
        extra = jnp.where(lane < 2, marks[slot][...], jnp.where(lane == 2, high, low))
        extras = []
        for part in range(parts):
            places = [source * vectors + part * 8 for source in range(sources)]
            block = jnp.concatenate([sums[at : at + 8, :width] for at in places], axis=0)
            out_ref[group * parts + part, :vectors, :] = block.astype(BF16)
            extras += [extra[at : at + 8, :] for at in places]
        extras_of[slot][...] = jnp.concatenate(extras, axis=0).astype(BF16)

    def emit(group, slot):
        pick = (iota((EXTRA, width), 0) == iota((EXTRA, width), 1)).astype(BF16)
        turned = lax.dot_general(
            pick, extras_of[slot][...], (((1,), (1,)), ((), ())), preferred_element_type=F32
        )
        for part in range(parts):
            at = part // 2 * width
            row = turned[:, at : at + width]
            if part % 2:
                row = pltpu.roll(row, vectors, 1)
            out_ref[group * parts + part, vectors:, :] = row.astype(BF16)

    def step(group, slot, late=True):
        mask(group - 1, 1 - slot)
        score(group, slot)
        finish(group - 1, 1 - slot)
        if late:
            emit(group - 2, slot)

    def pair(index, carry):
        step(2 * index, 0)
        step(2 * index + 1, 1)
        return carry

    score(0, 0)
    step(1, 1, late=False)
    lax.fori_loop(1, groups // 2, pair, 0)
    mask(groups - 1, 1)
    emit(groups - 2, 0)
    finish(groups - 1, 1)
    emit(groups - 1, 1)


def combine_kernel(in_ref, out_ref):
    places, total_rows, width = in_ref.shape
    vectors = total_rows - EXTRA
    extra = in_ref[:, vectors:, :].astype(F32).reshape(places * EXTRA, width).astype(BF16)
    unit = (iota((vectors, width), 0) == iota((vectors, width), 1)).astype(BF16)
    turned = lax.dot_general(unit, extra, (((1,), (1,)), ((), ())), preferred_element_type=F32)
    turned = turned.astype(BF16)
    column = iota((places * EXTRA, places), 0)
    wanted = iota((places * EXTRA, places), 1) * EXTRA

    def both_halves(index):
        pick = ((column == wanted + index) | (column == wanted + index + 1)).astype(BF16)
        return jnp.dot(turned, pick, preferred_element_type=F32)

    top = both_halves(0)
    total = both_halves(2)
    factor = jnp.exp2(top - jnp.max(top, axis=1, keepdims=True))
    denom = jnp.sum(factor * total, axis=1, keepdims=True)
    numer = jnp.zeros((vectors, width), F32)
    for at in range(places):
        numer = numer + factor[:, at : at + 1] * in_ref[at, :vectors, :].astype(F32)
    rotated = numer / denom
    common = iota((width, width), 0) & iota((width, width), 1)
    common = common ^ (common >> 4)
    common = common ^ (common >> 2)
    common = common ^ (common >> 1)
    signs = (1 - 2 * (common & 1)).astype(F32)
    attended = jnp.dot(rotated, signs, precision=lax.Precision.HIGHEST, preferred_element_type=F32)
    attended = (attended * (1.0 / math.sqrt(width))).astype(BF16)
    new = iota((vectors, vectors), 0)
    old = iota((vectors, vectors), 1)
    source = (new % 16) // 2
    pick = (old == source * 8 + (new // 16) * 2 + new % 2).astype(BF16)
    attended = jnp.dot(pick, attended, preferred_element_type=F32).astype(BF16)
    for at in range(places):
        out_ref[at] = attended


def project_kernel(in_ref, w_ref, out_ref):
    groups, pairs, vectors, width = in_ref.shape
    half = vectors // 2
    terms = jnp.zeros((groups * half, w_ref.shape[1]), F32)
    for pair in range(pairs):
        both = [
            in_ref[:, pair, at : at + half, :].reshape(groups * half, width) for at in (0, half)
        ]
        terms = terms + jnp.dot(
            jnp.concatenate(both, axis=1),
            w_ref[pair * 2 * width : (pair + 1) * 2 * width, :],
            preferred_element_type=F32,
        )
    out_ref[...] = terms.astype(BF16).reshape(out_ref.shape)


def local(queries, key_codes, key_scales, value_codes, value_scales, lengths, out_weight):
    steps, rows_own, heads, width = queries.shape
    tokens = key_codes.shape[1]
    places = lax.axis_size("ctx")
    groups = lax.axis_size("tp")
    sources = places // groups
    vectors = steps * rows_own * heads

    own = queries.transpose(2, 0, 1, 3).reshape(1, vectors, width)

    def direct(own):
        return lax.all_to_all(
            jnp.broadcast_to(own, (places, vectors, width)), "ctx", 0, 0, tiled=True
        )

    def two_stages(own):
        lines = [[at * sources + i for i in range(sources)] for at in range(groups)]
        across = [[i * sources + at for i in range(groups)] for at in range(sources)]
        line = lax.all_to_all(
            jnp.broadcast_to(own, (sources, vectors, width)),
            "ctx", 0, 0, axis_index_groups=lines, tiled=True,
        )
        line = line.reshape(1, sources * vectors, width)
        whole = lax.all_to_all(
            jnp.broadcast_to(line, (groups, sources * vectors, width)),
            "ctx", 0, 0, axis_index_groups=across, tiled=True,
        )
        return whole.reshape(places, vectors, width)

    def prepare(key_codes, key_scales, value_codes, value_scales):
        value = (value_codes[0].astype(F32) * value_scales[0][:, None]).astype(BF16)
        value = jnp.concatenate([value, jnp.ones_like(value)], axis=1)
        return key_codes[0].T, key_scales * (LOG2E / math.sqrt(width)), value

    def two_stages_first(own, memory):
        query, memory = lax.optimization_barrier((two_stages(own), memory))
        return query, prepare(*memory)

    memory = (key_codes, key_scales, value_codes, value_scales)
    query, (key_turned, key_factor, value) = lax.cond(
        lax.axis_index("tp") % 2 == 0,
        lambda own, memory: (direct(own), prepare(*memory)),
        two_stages_first,
        own,
        memory,
    )

    block = sources * vectors
    vmem = pl.BlockSpec(memory_space=pltpu.VMEM)
    partial = pl.pallas_call(
        attention_kernel,
        out_shape=jax.ShapeDtypeStruct((places, vectors + EXTRA, width), BF16),
        in_specs=[pl.BlockSpec(memory_space=pltpu.SMEM), vmem, vmem, vmem, vmem],
        out_specs=vmem,
        scratch_shapes=[pltpu.VMEM((block, tokens), F32)] * 2
        + [pltpu.VMEM((block, tokens), BF16)] * 2
        + [pltpu.VMEM((block, width), F32)] * 2
        + [pltpu.VMEM((block, width), BF16)] * 2,
        compiler_params=pltpu.CompilerParams(vmem_limit_bytes=48 * 1024 * 1024),
        cost_estimate=pl.CostEstimate(
            flops=8 * places * vectors * tokens * width,
            bytes_accessed=8 * 1024 * 1024,
            transcendentals=places * vectors * tokens,
        ),
        name="attention",
    )(lengths, query, key_turned, key_factor, value)

    pieces = lax.all_to_all(partial, "ctx", 0, 0, tiled=True)
    params = pltpu.CompilerParams(vmem_limit_bytes=32 * 1024 * 1024)
    attended = pl.pallas_call(
        combine_kernel,
        out_shape=jax.ShapeDtypeStruct((places, vectors, width), BF16),
        compiler_params=params,
        name="combine",
    )(pieces)
    attended = lax.all_to_all(attended, "ctx", 0, 0, tiled=True)
    half = vectors // 2
    terms = pl.pallas_call(
        project_kernel,
        out_shape=jax.ShapeDtypeStruct((groups, half, out_weight.shape[1]), BF16),
        compiler_params=params,
        name="project",
    )(attended.reshape(groups, sources, vectors, width), out_weight)
    terms = lax.all_to_all(terms, "tp", 0, 0, tiled=True)
    projected = jnp.sum(terms.astype(F32), axis=0).astype(BF16)
    return projected.reshape(steps, half // steps, out_weight.shape[1])


def solution(mesh):
    return jax.shard_map(
        local,
        mesh=mesh,
        in_specs=(
            P(None, "ctx", "tp", None),
            P("tp", "ctx", None),
            P("tp", "ctx"),
            P("tp", "ctx", None),
            P("tp", "ctx"),
            P(),
            P("tp", "ctx"),
        ),
        out_specs=P(None, "tp", "ctx"),
        check_vma=False,
    )
```

```python
import functools
import math

import jax
import jax.numpy as jnp
from jax import lax
from jax.experimental import pallas as pl
from jax.experimental.pallas import tpu as pltpu
from jax.sharding import PartitionSpec as P

F32 = jnp.float32
BF16 = jnp.bfloat16
LOG2E = 1.0 / math.log(2.0)
EXTRA = 8
NONE = -(2.0**100)


def split_two(x):
    high = x.astype(BF16).astype(F32)
    low = (x - high).astype(BF16).astype(F32)
    return high, low


def iota(shape, axis):
    return lax.broadcasted_iota(jnp.int32, shape, axis)


def attention_kernel(
    len_ref, q_ref, kt_ref, kf_ref, v_ref, out_ref,
    s_even, s_odd, p_even, p_odd, m_even, m_odd, e_even, e_odd,
):
    vectors, width = q_ref.shape[1:]
    tokens = kt_ref.shape[1]
    rows = s_even.shape[0]
    sources = rows // vectors
    groups = q_ref.shape[0] // sources
    parts = vectors // 8
    sub = 16
    start = lax.axis_index("ctx") * tokens
    scores, weights, marks = (s_even, s_odd), (p_even, p_odd), (m_even, m_odd)
    extras_of = (e_even, e_odd)

    def limits(group, source):
        row = (group * sources + source) * 2
        return len_ref[row] - start, len_ref[row + 1] - start

    def score(group, slot):
        q = q_ref[pl.ds(group * sources, sources)].reshape(rows, width)
        scores[slot][...] = jnp.dot(q, kt_ref[...], preferred_element_type=F32)

    def mask(group, slot):
        for source in range(sources):
            even, odd = limits(group, source)
            inside = ((even > 0) & (even < tokens)) | ((odd > 0) & (odd < tokens))

            @pl.when(inside)
            def _():
                first = jnp.where(even <= 0, tokens, even)
                second = jnp.where(odd <= 0, tokens, odd)
                limit = jnp.where(iota((sub, 1), 0) % 2 == 0, first, second)
                valid = iota((1, tokens), 1) < limit
                for at in range(source * vectors, (source + 1) * vectors, sub):
                    held = scores[slot][at : at + sub, :]
                    scores[slot][at : at + sub, :] = jnp.where(valid, held, NONE)

    def weigh(group, slot, half):
        kf = kf_ref[...]
        lane = iota((sub, width), 1)
        for at in range(half * rows // 2, (half + 1) * rows // 2, sub):
            even, odd = limits(group, at // vectors)
            some = jnp.where(iota((sub, 1), 0) % 2 == 0, even, odd) > 0
            scaled = scores[slot][at : at + sub, :] * kf
            high, low = split_two(jnp.max(scaled, axis=1, keepdims=True))
            weights[slot][at : at + sub, :] = jnp.exp2(scaled - (high + low)).astype(BF16)
            high = jnp.where(some, high, NONE)
            low = jnp.where(some, low, 0.0)
            marks[slot][at : at + sub, :] = jnp.where(lane == 0, high, low)

    def sums_of(slot, half):
        own = weights[slot][half * rows // 2 : (half + 1) * rows // 2, :]
        return jnp.dot(own, v_ref[...], preferred_element_type=F32)

    def finish(group, slot):
        weigh(group, slot, 0)
        first = sums_of(slot, 0)
        weigh(group, slot, 1)
        sums = jnp.concatenate([first, sums_of(slot, 1)], axis=0)
        high, low = split_two(sums[:, width:])
        lane = iota((rows, width), 1)
        extra = jnp.where(lane < 2, marks[slot][...], jnp.where(lane == 2, high, low))
        extras = []
        for part in range(parts):
            places = [source * vectors + part * 8 for source in range(sources)]
            block = jnp.concatenate([sums[at : at + 8, :width] for at in places], axis=0)
            out_ref[group * parts + part, :vectors, :] = block.astype(BF16)
            extras += [extra[at : at + 8, :] for at in places]
        extras_of[slot][...] = jnp.concatenate(extras, axis=0).astype(BF16)

    def emit(group, slot):
        pick = (iota((EXTRA, width), 0) == iota((EXTRA, width), 1)).astype(BF16)
        turned = lax.dot_general(
            pick, extras_of[slot][...], (((1,), (1,)), ((), ())), preferred_element_type=F32
        )
        for part in range(parts):
            at = part // 2 * width
            row = turned[:, at : at + width]
            if part % 2:
                row = pltpu.roll(row, vectors, 1)
            out_ref[group * parts + part, vectors:, :] = row.astype(BF16)

    def step(group, slot, late=True):
        mask(group - 1, 1 - slot)
        score(group, slot)
        finish(group - 1, 1 - slot)
        if late:
            emit(group - 2, slot)

    def pair(index, carry):
        step(2 * index, 0)
        step(2 * index + 1, 1)
        return carry

    score(0, 0)
    step(1, 1, late=False)
    lax.fori_loop(1, groups // 2, pair, 0)
    mask(groups - 1, 1)
    emit(groups - 2, 0)
    finish(groups - 1, 1)
    emit(groups - 1, 1)


def combine_kernel(in_ref, out_ref):
    places, total_rows, width = in_ref.shape
    vectors = total_rows - EXTRA
    extra = in_ref[:, vectors:, :].astype(F32).reshape(places * EXTRA, width).astype(BF16)
    unit = (iota((vectors, width), 0) == iota((vectors, width), 1)).astype(BF16)
    turned = lax.dot_general(unit, extra, (((1,), (1,)), ((), ())), preferred_element_type=F32)
    turned = turned.astype(BF16)
    column = iota((places * EXTRA, places), 0)
    wanted = iota((places * EXTRA, places), 1) * EXTRA

    def both_halves(index):
        pick = ((column == wanted + index) | (column == wanted + index + 1)).astype(BF16)
        return jnp.dot(turned, pick, preferred_element_type=F32)

    top = both_halves(0)
    total = both_halves(2)
    factor = jnp.exp2(top - jnp.max(top, axis=1, keepdims=True))
    denom = jnp.sum(factor * total, axis=1, keepdims=True)
    numer = jnp.zeros((vectors, width), F32)
    for at in range(places):
        numer = numer + factor[:, at : at + 1] * in_ref[at, :vectors, :].astype(F32)
    rotated = numer / denom
    common = iota((width, width), 0) & iota((width, width), 1)
    common = common ^ (common >> 4)
    common = common ^ (common >> 2)
    common = common ^ (common >> 1)
    signs = (1 - 2 * (common & 1)).astype(F32)
    attended = jnp.dot(rotated, signs, precision=lax.Precision.HIGHEST, preferred_element_type=F32)
    attended = (attended * (1.0 / math.sqrt(width))).astype(BF16)
    new = iota((vectors, vectors), 0)
    old = iota((vectors, vectors), 1)
    source = (new % 16) // 2
    pick = (old == source * 8 + (new // 16) * 2 + new % 2).astype(BF16)
    attended = jnp.dot(pick, attended, preferred_element_type=F32).astype(BF16)
    for at in range(places):
        out_ref[at] = attended


def project_kernel(in_ref, w_ref, out_ref):
    groups, pairs, vectors, width = in_ref.shape
    half = vectors // 2
    terms = jnp.zeros((groups * half, w_ref.shape[1]), F32)
    for pair in range(pairs):
        both = [
            in_ref[:, pair, at : at + half, :].reshape(groups * half, width) for at in (0, half)
        ]
        terms = terms + jnp.dot(
            jnp.concatenate(both, axis=1),
            w_ref[pair * 2 * width : (pair + 1) * 2 * width, :],
            preferred_element_type=F32,
        )
    out_ref[...] = terms.astype(BF16).reshape(out_ref.shape)


def local(queries, key_codes, key_scales, value_codes, value_scales, lengths, out_weight):
    steps, rows_own, heads, width = queries.shape
    tokens = key_codes.shape[1]
    places = lax.axis_size("ctx")
    groups = lax.axis_size("tp")
    sources = places // groups
    vectors = steps * rows_own * heads

    own = queries.transpose(2, 0, 1, 3).reshape(1, vectors, width)

    def direct(own):
        return lax.all_to_all(
            jnp.broadcast_to(own, (places, vectors, width)), "ctx", 0, 0, tiled=True
        )

    def two_stages(own):
        lines = [[at * sources + i for i in range(sources)] for at in range(groups)]
        across = [[i * sources + at for i in range(groups)] for at in range(sources)]
        line = lax.all_to_all(
            jnp.broadcast_to(own, (sources, vectors, width)),
            "ctx", 0, 0, axis_index_groups=lines, tiled=True,
        )
        line = line.reshape(1, sources * vectors, width)
        whole = lax.all_to_all(
            jnp.broadcast_to(line, (groups, sources * vectors, width)),
            "ctx", 0, 0, axis_index_groups=across, tiled=True,
        )
        return whole.reshape(places, vectors, width)

    def prepare(key_codes, key_scales, value_codes, value_scales):
        value = (value_codes[0].astype(F32) * value_scales[0][:, None]).astype(BF16)
        value = jnp.concatenate([value, jnp.ones_like(value)], axis=1)
        return key_codes[0].T, key_scales * (LOG2E / math.sqrt(width)), value

    def two_stages_first(own, memory):
        query, memory = lax.optimization_barrier((two_stages(own), memory))
        return query, prepare(*memory)

    memory = (key_codes, key_scales, value_codes, value_scales)
    query, (key_turned, key_factor, value) = lax.cond(
        lax.axis_index("tp") % 2 == 1,
        lambda own, memory: (direct(own), prepare(*memory)),
        two_stages_first,
        own,
        memory,
    )

    block = sources * vectors
    vmem = pl.BlockSpec(memory_space=pltpu.VMEM)
    partial = pl.pallas_call(
        attention_kernel,
        out_shape=jax.ShapeDtypeStruct((places, vectors + EXTRA, width), BF16),
        in_specs=[pl.BlockSpec(memory_space=pltpu.SMEM), vmem, vmem, vmem, vmem],
        out_specs=vmem,
        scratch_shapes=[pltpu.VMEM((block, tokens), F32)] * 2
        + [pltpu.VMEM((block, tokens), BF16)] * 2
        + [pltpu.VMEM((block, width), F32)] * 2
        + [pltpu.VMEM((block, width), BF16)] * 2,
        compiler_params=pltpu.CompilerParams(vmem_limit_bytes=48 * 1024 * 1024),
        cost_estimate=pl.CostEstimate(
            flops=8 * places * vectors * tokens * width,
            bytes_accessed=8 * 1024 * 1024,
            transcendentals=places * vectors * tokens,
        ),
        name="attention",
    )(lengths, query, key_turned, key_factor, value)

    pieces = lax.all_to_all(partial, "ctx", 0, 0, tiled=True)
    params = pltpu.CompilerParams(vmem_limit_bytes=32 * 1024 * 1024)
    attended = pl.pallas_call(
        combine_kernel,
        out_shape=jax.ShapeDtypeStruct((places, vectors, width), BF16),
        compiler_params=params,
        name="combine",
    )(pieces)
    attended = lax.all_to_all(attended, "ctx", 0, 0, tiled=True)
    half = vectors // 2
    terms = pl.pallas_call(
        project_kernel,
        out_shape=jax.ShapeDtypeStruct((groups, half, out_weight.shape[1]), BF16),
        compiler_params=params,
        name="project",
    )(attended.reshape(groups, sources, vectors, width), out_weight)
    terms = lax.all_to_all(terms, "tp", 0, 0, tiled=True)
    projected = jnp.sum(terms.astype(F32), axis=0).astype(BF16)
    return projected.reshape(steps, half // steps, out_weight.shape[1])


def solution(mesh):
    return jax.shard_map(
        local,
        mesh=mesh,
        in_specs=(
            P(None, "ctx", "tp", None),
            P("tp", "ctx", None),
            P("tp", "ctx"),
            P("tp", "ctx", None),
            P("tp", "ctx"),
            P(),
            P("tp", "ctx"),
        ),
        out_specs=P(None, "tp", "ctx"),
        check_vma=False,
    )
```

```python
import functools
import math

import jax
import jax.numpy as jnp
from jax import lax
from jax.experimental import pallas as pl
from jax.experimental.pallas import tpu as pltpu
from jax.sharding import PartitionSpec as P

F32 = jnp.float32
BF16 = jnp.bfloat16
LOG2E = 1.0 / math.log(2.0)
EXTRA = 8
NONE = -(2.0**100)


def split_two(x):
    high = x.astype(BF16).astype(F32)
    low = (x - high).astype(BF16).astype(F32)
    return high, low


def iota(shape, axis):
    return lax.broadcasted_iota(jnp.int32, shape, axis)


def attention_kernel(
    len_ref, q_ref, kt_ref, kf_ref, v_ref, out_ref,
    s_even, s_odd, p_even, p_odd, m_even, m_odd, e_even, e_odd,
):
    vectors, width = q_ref.shape[1:]
    tokens = kt_ref.shape[1]
    rows = s_even.shape[0]
    sources = rows // vectors
    groups = q_ref.shape[0] // sources
    parts = vectors // 8
    sub = 16
    start = lax.axis_index("ctx") * tokens
    scores, weights, marks = (s_even, s_odd), (p_even, p_odd), (m_even, m_odd)
    extras_of = (e_even, e_odd)

    def limits(group, source):
        row = (group * sources + source) * 2
        return len_ref[row] - start, len_ref[row + 1] - start

    def score(group, slot):
        q = q_ref[pl.ds(group * sources, sources)].reshape(rows, width)
        scores[slot][...] = jnp.dot(q, kt_ref[...], preferred_element_type=F32)

    def mask(group, slot):
        for source in range(sources):
            even, odd = limits(group, source)
            inside = ((even > 0) & (even < tokens)) | ((odd > 0) & (odd < tokens))

            @pl.when(inside)
            def _():
                first = jnp.where(even <= 0, tokens, even)
                second = jnp.where(odd <= 0, tokens, odd)
                limit = jnp.where(iota((sub, 1), 0) % 2 == 0, first, second)
                valid = iota((1, tokens), 1) < limit
                for at in range(source * vectors, (source + 1) * vectors, sub):
                    held = scores[slot][at : at + sub, :]
                    scores[slot][at : at + sub, :] = jnp.where(valid, held, NONE)

    def weigh(group, slot, half):
        kf = kf_ref[...]
        lane = iota((sub, width), 1)
        for at in range(half * rows // 2, (half + 1) * rows // 2, sub):
            even, odd = limits(group, at // vectors)
            some = jnp.where(iota((sub, 1), 0) % 2 == 0, even, odd) > 0
            scaled = scores[slot][at : at + sub, :] * kf
            high, low = split_two(jnp.max(scaled, axis=1, keepdims=True))
            weights[slot][at : at + sub, :] = jnp.exp2(scaled - (high + low)).astype(BF16)
            high = jnp.where(some, high, NONE)
            low = jnp.where(some, low, 0.0)
            marks[slot][at : at + sub, :] = jnp.where(lane == 0, high, low)

    def sums_of(slot, half):
        own = weights[slot][half * rows // 2 : (half + 1) * rows // 2, :]
        return jnp.dot(own, v_ref[...], preferred_element_type=F32)

    def finish(group, slot):
        weigh(group, slot, 0)
        first = sums_of(slot, 0)
        weigh(group, slot, 1)
        sums = jnp.concatenate([first, sums_of(slot, 1)], axis=0)
        high, low = split_two(sums[:, width:])
        lane = iota((rows, width), 1)
        extra = jnp.where(lane < 2, marks[slot][...], jnp.where(lane == 2, high, low))
        extras = []
        for part in range(parts):
            places = [source * vectors + part * 8 for source in range(sources)]
            block = jnp.concatenate([sums[at : at + 8, :width] for at in places], axis=0)
            out_ref[group * parts + part, :vectors, :] = block.astype(BF16)
            extras += [extra[at : at + 8, :] for at in places]
        extras_of[slot][...] = jnp.concatenate(extras, axis=0).astype(BF16)

    def emit(group, slot):
        pick = (iota((EXTRA, width), 0) == iota((EXTRA, width), 1)).astype(BF16)
        turned = lax.dot_general(
            pick, extras_of[slot][...], (((1,), (1,)), ((), ())), preferred_element_type=F32
        )
        for part in range(parts):
            at = part // 2 * width
            row = turned[:, at : at + width]
            if part % 2:
                row = pltpu.roll(row, vectors, 1)
            out_ref[group * parts + part, vectors:, :] = row.astype(BF16)

    def step(group, slot, late=True):
        mask(group - 1, 1 - slot)
        score(group, slot)
        finish(group - 1, 1 - slot)
        if late:
            emit(group - 2, slot)

    def pair(index, carry):
        step(2 * index, 0)
        step(2 * index + 1, 1)
        return carry

    score(0, 0)
    step(1, 1, late=False)
    lax.fori_loop(1, groups // 2, pair, 0)
    mask(groups - 1, 1)
    emit(groups - 2, 0)
    finish(groups - 1, 1)
    emit(groups - 1, 1)


def spread_kernel(in_ref, out_ref):
    steps, rows, heads, width = in_ref.shape
    vectors = steps * rows * heads
    new = iota((vectors, vectors), 0)
    old = iota((vectors, vectors), 1)
    pick = (old == new % (steps * rows) * heads + new // (steps * rows)).astype(BF16)
    own = in_ref[...].reshape(vectors, width)
    own = jnp.dot(pick, own, preferred_element_type=F32).astype(BF16)
    for at in range(out_ref.shape[0]):
        out_ref[at] = own


def combine_kernel(in_ref, out_ref):
    places, total_rows, width = in_ref.shape
    vectors = total_rows - EXTRA
    extra = in_ref[:, vectors:, :].astype(F32).reshape(places * EXTRA, width).astype(BF16)
    unit = (iota((vectors, width), 0) == iota((vectors, width), 1)).astype(BF16)
    turned = lax.dot_general(unit, extra, (((1,), (1,)), ((), ())), preferred_element_type=F32)
    turned = turned.astype(BF16)
    column = iota((places * EXTRA, places), 0)
    wanted = iota((places * EXTRA, places), 1) * EXTRA

    def both_halves(index):
        pick = ((column == wanted + index) | (column == wanted + index + 1)).astype(BF16)
        return jnp.dot(turned, pick, preferred_element_type=F32)

    top = both_halves(0)
    total = both_halves(2)
    factor = jnp.exp2(top - jnp.max(top, axis=1, keepdims=True))
    denom = jnp.sum(factor * total, axis=1, keepdims=True)
    numer = jnp.zeros((vectors, width), F32)
    for at in range(places):
        numer = numer + factor[:, at : at + 1] * in_ref[at, :vectors, :].astype(F32)
    rotated = numer / denom
    common = iota((width, width), 0) & iota((width, width), 1)
    common = common ^ (common >> 4)
    common = common ^ (common >> 2)
    common = common ^ (common >> 1)
    signs = (1 - 2 * (common & 1)).astype(BF16)
    attended = jnp.zeros((vectors, width), F32)
    rest = rotated
    for _ in range(3):
        piece = rest.astype(BF16)
        rest = rest - piece.astype(F32)
        attended = attended + jnp.dot(piece, signs, preferred_element_type=F32)
    attended = (attended * (1.0 / math.sqrt(width))).astype(BF16)
    new = iota((vectors, vectors), 0)
    old = iota((vectors, vectors), 1)
    source = (new % 16) // 2
    pick = (old == source * 8 + (new // 16) * 2 + new % 2).astype(BF16)
    attended = jnp.dot(pick, attended, preferred_element_type=F32).astype(BF16)
    for at in range(places):
        out_ref[at] = attended


def project_kernel(in_ref, w_ref, out_ref):
    groups, pairs, vectors, width = in_ref.shape
    half = vectors // 2
    terms = jnp.zeros((groups * half, w_ref.shape[1]), F32)
    for pair in range(pairs):
        both = [
            in_ref[:, pair, at : at + half, :].reshape(groups * half, width) for at in (0, half)
        ]
        terms = terms + jnp.dot(
            jnp.concatenate(both, axis=1),
            w_ref[pair * 2 * width : (pair + 1) * 2 * width, :],
            preferred_element_type=F32,
        )
    out_ref[...] = terms.astype(BF16).reshape(out_ref.shape)


def local(queries, key_codes, key_scales, value_codes, value_scales, lengths, out_weight):
    steps, rows_own, heads, width = queries.shape
    tokens = key_codes.shape[1]
    places = lax.axis_size("ctx")
    groups = lax.axis_size("tp")
    sources = places // groups
    vectors = steps * rows_own * heads

    own = queries.transpose(2, 0, 1, 3).reshape(1, vectors, width)

    def direct(own):
        return lax.all_to_all(
            jnp.broadcast_to(own, (places, vectors, width)), "ctx", 0, 0, tiled=True
        )

    def two_stages(own):
        lines = [[at * sources + i for i in range(sources)] for at in range(groups)]
        across = [[i * sources + at for i in range(groups)] for at in range(sources)]
        line = lax.all_to_all(
            pl.pallas_call(
                spread_kernel,
                out_shape=jax.ShapeDtypeStruct((sources, vectors, width), BF16),
                name="spread",
            )(queries),
            "ctx", 0, 0, axis_index_groups=lines, tiled=True,
        )
        line = line.reshape(1, sources * vectors, width)
        whole = lax.all_to_all(
            jnp.broadcast_to(line, (groups, sources * vectors, width)),
            "ctx", 0, 0, axis_index_groups=across, tiled=True,
        )
        return whole.reshape(places, vectors, width)

    def prepare(key_codes, key_scales, value_codes, value_scales):
        value = (value_codes[0].astype(F32) * value_scales[0][:, None]).astype(BF16)
        value = jnp.concatenate([value, jnp.ones_like(value)], axis=1)
        return key_codes[0].T, key_scales * (LOG2E / math.sqrt(width)), value

    def two_stages_first(own, memory):
        query, memory = lax.optimization_barrier((two_stages(own), memory))
        return query, prepare(*memory)

    memory = (key_codes, key_scales, value_codes, value_scales)
    query, (key_turned, key_factor, value) = lax.cond(
        lax.axis_index("tp") % 2 == 1,
        lambda own, memory: (direct(own), prepare(*memory)),
        two_stages_first,
        own,
        memory,
    )

    block = sources * vectors
    vmem = pl.BlockSpec(memory_space=pltpu.VMEM)
    partial = pl.pallas_call(
        attention_kernel,
        out_shape=jax.ShapeDtypeStruct((places, vectors + EXTRA, width), BF16),
        in_specs=[pl.BlockSpec(memory_space=pltpu.SMEM), vmem, vmem, vmem, vmem],
        out_specs=vmem,
        scratch_shapes=[pltpu.VMEM((block, tokens), F32)] * 2
        + [pltpu.VMEM((block, tokens), BF16)] * 2
        + [pltpu.VMEM((block, width), F32)] * 2
        + [pltpu.VMEM((block, width), BF16)] * 2,
        compiler_params=pltpu.CompilerParams(vmem_limit_bytes=48 * 1024 * 1024),
        cost_estimate=pl.CostEstimate(
            flops=8 * places * vectors * tokens * width,
            bytes_accessed=8 * 1024 * 1024,
            transcendentals=places * vectors * tokens,
        ),
        name="attention",
    )(lengths, query, key_turned, key_factor, value)

    pieces = lax.all_to_all(partial, "ctx", 0, 0, tiled=True)
    params = pltpu.CompilerParams(vmem_limit_bytes=32 * 1024 * 1024)
    attended = pl.pallas_call(
        combine_kernel,
        out_shape=jax.ShapeDtypeStruct((places, vectors, width), BF16),
        compiler_params=params,
        name="combine",
    )(pieces)
    attended = lax.all_to_all(attended, "ctx", 0, 0, tiled=True)
    half = vectors // 2
    terms = pl.pallas_call(
        project_kernel,
        out_shape=jax.ShapeDtypeStruct((groups, half, out_weight.shape[1]), BF16),
        compiler_params=params,
        name="project",
    )(attended.reshape(groups, sources, vectors, width), out_weight)
    terms = lax.all_to_all(terms, "tp", 0, 0, tiled=True)
    projected = jnp.sum(terms.astype(F32), axis=0).astype(BF16)
    return projected.reshape(steps, half // steps, out_weight.shape[1])


def solution(mesh):
    return jax.shard_map(
        local,
        mesh=mesh,
        in_specs=(
            P(None, "ctx", "tp", None),
            P("tp", "ctx", None),
            P("tp", "ctx"),
            P("tp", "ctx", None),
            P("tp", "ctx"),
            P(),
            P("tp", "ctx"),
        ),
        out_specs=P(None, "tp", "ctx"),
        check_vma=False,
    )
```

```python
import functools
import math

import jax
import jax.numpy as jnp
from jax import lax
from jax.experimental import pallas as pl
from jax.experimental.pallas import tpu as pltpu
from jax.sharding import PartitionSpec as P

F32 = jnp.float32
BF16 = jnp.bfloat16
LOG2E = 1.0 / math.log(2.0)
EXTRA = 8
NONE = -(2.0**100)


def split_two(x):
    high = x.astype(BF16).astype(F32)
    low = (x - high).astype(BF16).astype(F32)
    return high, low


def iota(shape, axis):
    return lax.broadcasted_iota(jnp.int32, shape, axis)


def attention_kernel(
    len_ref, q_ref, kt_ref, kf_ref, v_ref, out_ref,
    s_even, s_odd, p_even, p_odd, m_even, m_odd, e_even, e_odd,
):
    vectors, width = q_ref.shape[1:]
    tokens = kt_ref.shape[1]
    rows = s_even.shape[0]
    sources = rows // vectors
    groups = q_ref.shape[0] // sources
    parts = vectors // 8
    sub = 32
    start = lax.axis_index("ctx") * tokens
    scores, weights, marks = (s_even, s_odd), (p_even, p_odd), (m_even, m_odd)
    extras_of = (e_even, e_odd)

    def limits(group, source):
        row = (group * sources + source) * 2
        return len_ref[row] - start, len_ref[row + 1] - start

    def score(group, slot):
        q = q_ref[pl.ds(group * sources, sources)].reshape(rows, width)
        scores[slot][...] = jnp.dot(q, kt_ref[...], preferred_element_type=F32)

    def mask(group, slot):
        for source in range(sources):
            even, odd = limits(group, source)
            inside = ((even > 0) & (even < tokens)) | ((odd > 0) & (odd < tokens))

            @pl.when(inside)
            def _():
                first = jnp.where(even <= 0, tokens, even)
                second = jnp.where(odd <= 0, tokens, odd)
                limit = jnp.where(iota((sub, 1), 0) % 2 == 0, first, second)
                valid = iota((1, tokens), 1) < limit
                for at in range(source * vectors, (source + 1) * vectors, sub):
                    held = scores[slot][at : at + sub, :]
                    scores[slot][at : at + sub, :] = jnp.where(valid, held, NONE)

    def weigh(group, slot, half):
        kf = kf_ref[...]
        lane = iota((sub, width), 1)
        for at in range(half * rows // 2, (half + 1) * rows // 2, sub):
            even, odd = limits(group, at // vectors)
            some = jnp.where(iota((sub, 1), 0) % 2 == 0, even, odd) > 0
            scaled = scores[slot][at : at + sub, :] * kf
            high, low = split_two(jnp.max(scaled, axis=1, keepdims=True))
            weights[slot][at : at + sub, :] = jnp.exp2(scaled - (high + low)).astype(BF16)
            high = jnp.where(some, high, NONE)
            low = jnp.where(some, low, 0.0)
            marks[slot][at : at + sub, :] = jnp.where(lane == 0, high, low)

    def sums_of(slot, half):
        own = weights[slot][half * rows // 2 : (half + 1) * rows // 2, :]
        return jnp.dot(own, v_ref[...], preferred_element_type=F32)

    def finish(group, slot):
        weigh(group, slot, 0)
        first = sums_of(slot, 0)
        weigh(group, slot, 1)
        sums = jnp.concatenate([first, sums_of(slot, 1)], axis=0)
        high, low = split_two(sums[:, width:])
        lane = iota((rows, width), 1)
        extra = jnp.where(lane < 2, marks[slot][...], jnp.where(lane == 2, high, low))
        extras = []
        for part in range(parts):
            places = [source * vectors + part * 8 for source in range(sources)]
            block = jnp.concatenate([sums[at : at + 8, :width] for at in places], axis=0)
            out_ref[group * parts + part, :vectors, :] = block.astype(BF16)
            extras += [extra[at : at + 8, :] for at in places]
        extras_of[slot][...] = jnp.concatenate(extras, axis=0).astype(BF16)

    def emit(group, slot):
        pick = (iota((EXTRA, width), 0) == iota((EXTRA, width), 1)).astype(BF16)
        turned = lax.dot_general(
            pick, extras_of[slot][...], (((1,), (1,)), ((), ())), preferred_element_type=F32
        )
        for part in range(parts):
            at = part // 2 * width
            row = turned[:, at : at + width]
            if part % 2:
                row = pltpu.roll(row, vectors, 1)
            out_ref[group * parts + part, vectors:, :] = row.astype(BF16)

    def step(group, slot, late=True):
        mask(group - 1, 1 - slot)
        score(group, slot)
        finish(group - 1, 1 - slot)
        if late:
            emit(group - 2, slot)

    def pair(index, carry):
        step(2 * index, 0)
        step(2 * index + 1, 1)
        return carry

    score(0, 0)
    step(1, 1, late=False)
    lax.fori_loop(1, groups // 2, pair, 0)
    mask(groups - 1, 1)
    emit(groups - 2, 0)
    finish(groups - 1, 1)
    emit(groups - 1, 1)


def spread_kernel(in_ref, out_ref):
    steps, rows, heads, width = in_ref.shape
    vectors = steps * rows * heads
    new = iota((vectors, vectors), 0)
    old = iota((vectors, vectors), 1)
    pick = (old == new % (steps * rows) * heads + new // (steps * rows)).astype(BF16)
    own = in_ref[...].reshape(vectors, width)
    own = jnp.dot(pick, own, preferred_element_type=F32).astype(BF16)
    for at in range(out_ref.shape[0]):
        out_ref[at] = own


def combine_kernel(in_ref, out_ref):
    places, total_rows, width = in_ref.shape
    vectors = total_rows - EXTRA
    extra = in_ref[:, vectors:, :].astype(F32).reshape(places * EXTRA, width).astype(BF16)
    unit = (iota((vectors, width), 0) == iota((vectors, width), 1)).astype(BF16)
    turned = lax.dot_general(unit, extra, (((1,), (1,)), ((), ())), preferred_element_type=F32)
    turned = turned.astype(BF16)
    column = iota((places * EXTRA, places), 0)
    wanted = iota((places * EXTRA, places), 1) * EXTRA

    def both_halves(index):
        pick = ((column == wanted + index) | (column == wanted + index + 1)).astype(BF16)
        return jnp.dot(turned, pick, preferred_element_type=F32)

    top = both_halves(0)
    total = both_halves(2)
    factor = jnp.exp2(top - jnp.max(top, axis=1, keepdims=True))
    denom = jnp.sum(factor * total, axis=1, keepdims=True)
    numer = jnp.zeros((vectors, width), F32)
    for at in range(places):
        numer = numer + factor[:, at : at + 1] * in_ref[at, :vectors, :].astype(F32)
    rotated = numer / denom
    common = iota((width, width), 0) & iota((width, width), 1)
    common = common ^ (common >> 4)
    common = common ^ (common >> 2)
    common = common ^ (common >> 1)
    signs = (1 - 2 * (common & 1)).astype(BF16)
    attended = jnp.zeros((vectors, width), F32)
    rest = rotated
    for _ in range(3):
        piece = rest.astype(BF16)
        rest = rest - piece.astype(F32)
        attended = attended + jnp.dot(piece, signs, preferred_element_type=F32)
    attended = (attended * (1.0 / math.sqrt(width))).astype(BF16)
    new = iota((vectors, vectors), 0)
    old = iota((vectors, vectors), 1)
    source = (new % 16) // 2
    pick = (old == source * 8 + (new // 16) * 2 + new % 2).astype(BF16)
    attended = jnp.dot(pick, attended, preferred_element_type=F32).astype(BF16)
    for at in range(places):
        out_ref[at] = attended


def project_kernel(in_ref, w_ref, out_ref):
    groups, pairs, vectors, width = in_ref.shape
    half = vectors // 2
    terms = jnp.zeros((groups * half, w_ref.shape[1]), F32)
    for pair in range(pairs):
        both = [
            in_ref[:, pair, at : at + half, :].reshape(groups * half, width) for at in (0, half)
        ]
        terms = terms + jnp.dot(
            jnp.concatenate(both, axis=1),
            w_ref[pair * 2 * width : (pair + 1) * 2 * width, :],
            preferred_element_type=F32,
        )
    out_ref[...] = terms.astype(BF16).reshape(out_ref.shape)


def local(queries, key_codes, key_scales, value_codes, value_scales, lengths, out_weight):
    steps, rows_own, heads, width = queries.shape
    tokens = key_codes.shape[1]
    places = lax.axis_size("ctx")
    groups = lax.axis_size("tp")
    sources = places // groups
    vectors = steps * rows_own * heads

    own = queries.transpose(2, 0, 1, 3).reshape(1, vectors, width)

    def direct(own):
        return lax.all_to_all(
            jnp.broadcast_to(own, (places, vectors, width)), "ctx", 0, 0, tiled=True
        )

    def two_stages(own):
        lines = [[at * sources + i for i in range(sources)] for at in range(groups)]
        across = [[i * sources + at for i in range(groups)] for at in range(sources)]
        line = lax.all_to_all(
            pl.pallas_call(
                spread_kernel,
                out_shape=jax.ShapeDtypeStruct((sources, vectors, width), BF16),
                name="spread",
            )(queries),
            "ctx", 0, 0, axis_index_groups=lines, tiled=True,
        )
        line = line.reshape(1, sources * vectors, width)
        whole = lax.all_to_all(
            jnp.broadcast_to(line, (groups, sources * vectors, width)),
            "ctx", 0, 0, axis_index_groups=across, tiled=True,
        )
        return whole.reshape(places, vectors, width)

    def prepare(key_codes, key_scales, value_codes, value_scales):
        value = (value_codes[0].astype(F32) * value_scales[0][:, None]).astype(BF16)
        value = jnp.concatenate([value, jnp.ones_like(value)], axis=1)
        return key_codes[0].T, key_scales * (LOG2E / math.sqrt(width)), value

    def two_stages_first(own, memory):
        query, memory = lax.optimization_barrier((two_stages(own), memory))
        return query, prepare(*memory)

    memory = (key_codes, key_scales, value_codes, value_scales)
    query, (key_turned, key_factor, value) = lax.cond(
        lax.axis_index("tp") % 2 == 1,
        lambda own, memory: (direct(own), prepare(*memory)),
        two_stages_first,
        own,
        memory,
    )

    block = sources * vectors
    vmem = pl.BlockSpec(memory_space=pltpu.VMEM)
    partial = pl.pallas_call(
        attention_kernel,
        out_shape=jax.ShapeDtypeStruct((places, vectors + EXTRA, width), BF16),
        in_specs=[pl.BlockSpec(memory_space=pltpu.SMEM), vmem, vmem, vmem, vmem],
        out_specs=vmem,
        scratch_shapes=[pltpu.VMEM((block, tokens), F32)] * 2
        + [pltpu.VMEM((block, tokens), BF16)] * 2
        + [pltpu.VMEM((block, width), F32)] * 2
        + [pltpu.VMEM((block, width), BF16)] * 2,
        compiler_params=pltpu.CompilerParams(vmem_limit_bytes=48 * 1024 * 1024),
        cost_estimate=pl.CostEstimate(
            flops=8 * places * vectors * tokens * width,
            bytes_accessed=8 * 1024 * 1024,
            transcendentals=places * vectors * tokens,
        ),
        name="attention",
    )(lengths, query, key_turned, key_factor, value)

    pieces = lax.all_to_all(partial, "ctx", 0, 0, tiled=True)
    params = pltpu.CompilerParams(vmem_limit_bytes=32 * 1024 * 1024)
    attended = pl.pallas_call(
        combine_kernel,
        out_shape=jax.ShapeDtypeStruct((places, vectors, width), BF16),
        compiler_params=params,
        name="combine",
    )(pieces)
    attended = lax.all_to_all(attended, "ctx", 0, 0, tiled=True)
    half = vectors // 2
    terms = pl.pallas_call(
        project_kernel,
        out_shape=jax.ShapeDtypeStruct((groups, half, out_weight.shape[1]), BF16),
        compiler_params=params,
        name="project",
    )(attended.reshape(groups, sources, vectors, width), out_weight)
    terms = lax.all_to_all(terms, "tp", 0, 0, tiled=True)
    projected = jnp.sum(terms.astype(F32), axis=0).astype(BF16)
    return projected.reshape(steps, half // steps, out_weight.shape[1])


def solution(mesh):
    return jax.shard_map(
        local,
        mesh=mesh,
        in_specs=(
            P(None, "ctx", "tp", None),
            P("tp", "ctx", None),
            P("tp", "ctx"),
            P("tp", "ctx", None),
            P("tp", "ctx"),
            P(),
            P("tp", "ctx"),
        ),
        out_specs=P(None, "tp", "ctx"),
        check_vma=False,
    )
```
